256 devices in a mesh: pipe: 32 (over x, z_hi, y), tensor: 4 (over z_lo), dp: 2 (over core).
Axes of the slice: x: 4, y: 4, z: 8 (z_hi: 2, z_lo: 4; z = z_hi * 4 + z_lo), core: 2. Of those that a mesh axis runs over, the one named last changes fastest.
Arguments:
- hidden: bfloat16 [512, 5120], P('dp', ('pipe', 'tensor')), may hold values from -16 to 16
- head_weight: bfloat16 [151936, 5120], P(('pipe', 'tensor'), 'dp'), may hold values from -2 to 2
- labels: int32 [512], P('dp'), may hold values from 0 to 151935
- loss_weight: float32 [512], P('dp'), may hold values from 1 to 10
Outputs:
- hidden_grad: bfloat16 [512, 5120], P('dp', ('pipe', 'tensor'))
- head_grad: bfloat16 [151936, 5120], P(('pipe', 'tensor'), 'dp')
- token_loss: float32 [512], P('dp')
The draws below stay inside these ranges and needn't reach their ends.
All inputs are finite; a program needn't handle non-finite values.
Results may differ from the reference program's by a relative error of at most 0.0052.
Values may be sent and summed in bfloat16 or wider, within the bound.
No kernel may reach another device: no remote copies, remote signals or barrier semaphores. Data moves between devices by JAX's collectives and lax.ppermute only.
A program may use at most 128 MiB of HBM per device.

```python
import math
import jax
import jax.numpy as jnp
from jax import lax

D = 5120
VOC_DEV = 1187
VOCAB = 151936
TOKENS = 512
N_PIPE = 32
N_TENSOR = 4


def row_keys(base_key, vocab_rows):
    return jax.vmap(lambda index: jax.random.fold_in(base_key, index))(vocab_rows)


def row_scale(base_key, vocab_rows):
    keys = row_keys(base_key, vocab_rows)
    spread = jax.vmap(lambda row_key: jax.random.uniform(jax.random.fold_in(row_key, 1), ()))(keys)
    rising = 1.0 + 2.0 * vocab_rows.astype(jnp.float32) / (VOCAB - 1)
    return jnp.exp(spread * math.log(10.0)) * rising


def shared_direction(base_key):
    common_key = jax.random.fold_in(base_key, 2)
    return jnp.clip(jax.random.normal(common_key, (D,)), -4.0, 4.0)


def normal_rows(base_key, vocab_rows):
    keys = row_keys(base_key, vocab_rows)
    return jax.vmap(lambda row_key: jnp.clip(jax.random.normal(row_key, (D,)), -5.0, 5.0))(keys)


def shaped_rows(base_key, vocab_rows, unit_rows):
    common = shared_direction(base_key)
    mixed = 0.6 * common[None, :] + 0.8 * unit_rows
    return mixed * (row_scale(base_key, vocab_rows) / math.sqrt(D))[:, None]


def draw_head_weight(key, part):
    key = jax.random.fold_in(key, 11)
    vocab_rows = jnp.arange(VOCAB, dtype=jnp.int32)
    unit_rows = normal_rows(key, vocab_rows)
    values = shaped_rows(key, vocab_rows, unit_rows)
    return jnp.clip(values, -2.0, 2.0).astype(jnp.bfloat16)


def draw_hidden(key, part):
    key = jax.random.fold_in(key, 23)
    scale_key = jax.random.fold_in(key, 0)
    values_key = jax.random.fold_in(key, 2)
    flat_key = jax.random.fold_in(key, 4)
    row_spread = 0.3 * jnp.exp(jax.random.uniform(scale_key, (TOKENS, 1)) * math.log(10.0))
    flat_rows = jax.random.uniform(flat_key, (TOKENS, 1)) < 0.12
    row_spread = jnp.where(flat_rows, 0.01, row_spread)
    values = row_spread * jnp.clip(jax.random.normal(values_key, (TOKENS, D)), -4.0, 4.0)
    return jnp.clip(values, -16.0, 16.0).astype(jnp.bfloat16)


def set_ends(values, stream_key, smallest, largest):
    index_at = [jax.random.randint(jax.random.fold_in(stream_key, axis), (), 0, length) for axis, length in enumerate(values.shape)]
    widest = values.shape.index(max(values.shape))
    next_to = index_at[:widest] + [(index_at[widest] + 1) % values.shape[widest]] + index_at[widest + 1:]
    return values.at[tuple(index_at)].set(smallest).at[tuple(next_to)].set(largest)


def levels(rng, shape, shards, least, top_value):
    gain = 1.0
    for position, shards_of in shards:
        steps = jax.random.uniform(jax.random.fold_in(jax.random.fold_in(rng, 6), position), (shards_of,), jnp.float32, least / len(shards), top_value / len(shards))
        gain = gain * jnp.repeat(jnp.exp(steps), shape[position] // shards_of).reshape((-1,) + (1,) * (len(shape) - 1 - position))
    return gain


def setup_inputs(seed: int = 0) -> dict:
    splits = jax.random.split(jax.random.key(seed), 5)
    return {
        "hidden": draw_hidden(jax.random.fold_in(splits[4], 71), 0),
        "head_weight": draw_head_weight(jax.random.fold_in(splits[4], 71), 0),
        "labels": set_ends(jax.random.randint(splits[2], (TOKENS,), 0, VOCAB), jax.random.fold_in(splits[2], 1), 0, VOCAB - 1).astype(jnp.int32),
        "loss_weight": jnp.clip(jnp.exp(math.log(10.0) - 2.3025851 * jax.random.uniform(splits[3], (TOKENS,), jnp.float32) ** levels(splits[3], (TOKENS,), ((0, 2),), -0.2, 0.2)), 1.0, 10.0),
    }


def reference(hidden, head_weight, labels, loss_weight):
    logits = lax.dot_general(hidden, head_weight, (((1,), (1,)), ((), ())), preferred_element_type=jnp.float32)
    row_peak = lax.optimization_barrier(jnp.max(logits, axis=1, keepdims=True))
    shifted_exp = jnp.exp(logits - row_peak)
    row_total = lax.optimization_barrier(jnp.sum(shifted_exp, axis=1, keepdims=True))
    vocab_rows = jnp.arange(logits.shape[1], dtype=jnp.int32)
    target_mask = (vocab_rows[None, :] == labels[:, None]).astype(jnp.float32)
    picked = lax.optimization_barrier(jnp.sum(target_mask * logits, axis=1))
    token_loss = row_peak[:, 0] + jnp.log(row_total[:, 0]) - picked
    logit_grad = (loss_weight[:, None] * (shifted_exp / row_total - target_mask)).astype(jnp.bfloat16)
    hidden_grad = jnp.dot(logit_grad, head_weight, preferred_element_type=jnp.float32).astype(jnp.bfloat16)
    blocks = logit_grad.T.reshape(N_PIPE * N_TENSOR, VOC_DEV, TOKENS)

    def block_grad(block):
        return jnp.dot(block, hidden, preferred_element_type=jnp.float32).astype(jnp.bfloat16)
    head_grad = lax.map(block_grad, blocks).reshape(VOCAB, D)
    return (hidden_grad, head_grad, token_loss)
```

```python
import jax
import jax.numpy as jnp
from jax import lax
from jax.sharding import Mesh, PartitionSpec as P


def ring(n, k):
    return [(i, (i + k) % n) for i in range(n)]


def gather_ring(block, axis):
    n = lax.axis_size(axis)
    me = lax.axis_index(axis)
    out = jnp.zeros((n,) + block.shape, block.dtype)
    got = {k: lax.ppermute(block, axis, ring(n, k)) for k in ((2, 1, 3) if n == 4 else (1,))}
    got[0] = block
    for k in range(n):
        out = lax.dynamic_update_index_in_dim(out, got[k], (me - k) % n, 0)
    return out


def scatter_ring(blocks, axis, dtype):
    n = lax.axis_size(axis)
    me = lax.axis_index(axis)
    pick = lambda k: lax.dynamic_index_in_dim(blocks, (me + k) % n, 0, keepdims=False)
    got = [lax.ppermute(pick(k).astype(dtype), axis, ring(n, k)) for k in ((2, 1, 3) if n == 4 else (1,))]
    total = pick(0).astype(jnp.float32)
    for piece in got:
        total = total + piece.astype(jnp.float32)
    return total


def merge(stats, axes):
    n = lax.axis_size(axes)
    every = lax.all_to_all(jnp.broadcast_to(stats[None], (n,) + stats.shape), axes, 0, 0)
    peak = jnp.max(every[:, 0], axis=0)
    total = jnp.sum(every[:, 1] * jnp.exp(every[:, 0] - peak[None]), axis=0)
    return jnp.stack([peak, total, jnp.sum(every[:, 2], axis=0)])


def per_device(hidden, head_weight, labels, loss_weight):
    bf = jnp.bfloat16
    f32 = jnp.float32
    rows, half = head_weight.shape
    swap = [(0, 1), (1, 0)]
    core = lax.axis_index("dp")
    tokens = hidden.shape[0]
    weight_other = lax.ppermute(head_weight, "dp", swap)

    cols = hidden.shape[1]
    block = gather_ring(hidden.T, "zh")
    block = gather_ring(block, "t")
    block = block.transpose(1, 0, 2, 3).reshape(2, 4 * cols, tokens)
    side = 2 * cols
    first = gather_ring(gather_ring(block[:, :side], "x"), "y")
    second = gather_ring(gather_ring(block[:, side:], "y"), "x")
    feats = jnp.stack([first.transpose(1, 2, 0, 3, 4), second.transpose(0, 2, 1, 3, 4)], axis=3)
    feats = feats.reshape(2, half, tokens)
    feats_own = lax.dynamic_index_in_dim(feats, core, 0, keepdims=False)
    feats_other = lax.dynamic_index_in_dim(feats, 1 - core, 0, keepdims=False)
    feats_peer = lax.ppermute(feats_other, "dp", swap)

    dot = lambda a, b, ca, cb: lax.dot_general(
        a, b, (((ca,), (cb,)), ((), ())), preferred_element_type=f32
    )
    logits = dot(head_weight, feats_own, 1, 0) + dot(weight_other, feats_other, 1, 0)
    first_entry = lax.axis_index(("x", "zh", "y", "t")) * rows
    vocab_rows = first_entry + jnp.arange(rows, dtype=jnp.int32)
    target = vocab_rows[:, None] == labels[None, :]
    peak = jnp.max(logits, axis=0)
    total = jnp.sum(jnp.exp(logits - peak[None, :]), axis=0)
    picked = jnp.sum(jnp.where(target, logits, 0.0), axis=0)
    stats = merge(merge(jnp.stack([peak, total, picked]), ("y", "t")), ("x", "zh"))
    peak, total, picked = stats[0], stats[1], stats[2]
    token_loss = peak + jnp.log(total) - picked
    grad = loss_weight[None, :] * (
        jnp.exp(logits - peak[None, :]) / total[None, :] - target.astype(f32)
    )
    grad = grad.astype(bf)
    grad_peer = lax.ppermute(grad, "dp", swap)

    own_part = dot(head_weight, grad, 0, 0).astype(bf)
    other_part = dot(weight_other, grad, 0, 0).astype(bf)
    parts = jnp.zeros((2, half, tokens), bf)
    parts = lax.dynamic_update_index_in_dim(parts, own_part, core, 0)
    parts = lax.dynamic_update_index_in_dim(parts, other_part, 1 - core, 0)
    parts = parts.reshape(4, 2, 4, 2, side, tokens)
    first = parts[:, :, :, 0].transpose(2, 0, 1, 3, 4)
    second = parts[:, :, :, 1].transpose(0, 2, 1, 3, 4)
    first = scatter_ring(scatter_ring(first, "y", bf), "x", bf)
    second = scatter_ring(scatter_ring(second, "x", bf), "y", bf)
    rest = jnp.concatenate([first, second], axis=1).reshape(2, 4, cols, tokens).transpose(1, 0, 2, 3)
    rest = scatter_ring(rest, "t", f32)
    hidden_grad = scatter_ring(rest, "zh", f32).astype(bf).T

    head_grad = dot(grad, feats_own, 1, 1) + dot(grad_peer, feats_peer, 1, 1)
    return (hidden_grad, head_grad.astype(bf), token_loss)


def solution(mesh):
    fine = Mesh(mesh.devices.reshape(4, 2, 4, 4, 2), ("x", "zh", "y", "t", "dp"))
    sections = ("x", "zh", "y", "t")
    return jax.shard_map(
        per_device,
        mesh=fine,
        in_specs=(P("dp", sections), P(sections, "dp"), P("dp"), P("dp")),
        out_specs=(P("dp", sections), P(sections, "dp"), P("dp")),
        check_vma=False,
    )
```

```python
import jax
import jax.numpy as jnp
from jax import lax
from jax.experimental import pallas as pl
from jax.experimental.pallas import tpu as pltpu
from jax.sharding import Mesh, PartitionSpec as P

BF = jnp.bfloat16
F32 = jnp.float32
HBM = pl.BlockSpec(memory_space=pltpu.HBM)
VMEM = pl.BlockSpec(memory_space=pltpu.VMEM)
SMEM = pl.BlockSpec(memory_space=pltpu.SMEM)
SECTIONS = ("x", "zh", "y", "t")


def paired(n, k):
    return [(i, i ^ k) for i in range(n)]


def spread(block, axis):
    got = {k: lax.ppermute(block, axis, paired(4, k)) for k in (2, 1, 3)}
    got[0] = block
    return [got[k] for k in range(4)]


def collect(blocks, axis):
    got = [lax.ppermute(blocks[k], axis, paired(4, k)) for k in (2, 1, 3)]
    total = blocks[0].astype(F32)
    for piece in got:
        total = total + piece.astype(F32)
    return total


def share(block, axes):
    n = lax.axis_size(axes)
    return lax.all_to_all(jnp.broadcast_to(block[None], (n,) + block.shape), axes, 0, 0)


def combine(every):
    peak = jnp.max(every[:, 0], axis=0)
    total = jnp.sum(every[:, 1] * jnp.exp(every[:, 0] - peak[None]), axis=0)
    return jnp.stack([peak, total, jnp.sum(every[:, 2], axis=0)])


def each_piece(pos, side, firsts, seconds, own, other, act):
    core, x, y = pos[0], pos[1], pos[2]
    for kx in range(4):
        place = x ^ kx ^ (2 * core)

        def visit(half):
            for zh in range(2):
                for ky in range(4):
                    block = ((place % 2) * 2 + zh) * 4 + (y ^ ky)
                    row = pl.multiple_of(block * 2 * side, 16)
                    act(firsts[ky], (kx, zh), half, pl.ds(row, side))
                    row = pl.multiple_of(block * 2 * side + side, 16)
                    act(seconds[kx], (ky, zh), half, pl.ds(row, side))

        pl.when(place < 2)(lambda: visit(own))
        pl.when(place >= 2)(lambda: visit(other))


def fetch(own_far, other_far, own, other, sems):
    copies = [
        pltpu.make_async_copy(own_far, own, sems.at[0]),
        pltpu.make_async_copy(other_far, other, sems.at[1]),
    ]
    for copy in copies:
        copy.start()
    return copies


def logits_kernel(pos, own_far, other_far, labels, a0, a1, a2, a3, b0, b1, b2, b3,
                  logits, stats, feats_own, feats_other, own, other, sems):
    copies = fetch(own_far, other_far, own, other, sems)

    def place(piece, index, half, rows):
        half[rows, :] = piece[index]

    firsts, seconds = (a0, a1, a2, a3), (b0, b1, b2, b3)
    each_piece(pos, a0.shape[2], firsts, seconds, feats_own, feats_other, place)
    copies[0].wait()
    logits[...] = jnp.dot(own[...], feats_own[...], preferred_element_type=F32)
    copies[1].wait()
    logits[...] += jnp.dot(other[...], feats_other[...], preferred_element_type=F32)
    value = logits[...]
    rows = lax.broadcasted_iota(jnp.int32, value.shape, 0) + pos[3]
    peak = jnp.max(value, axis=0, keepdims=True)
    stats[0:1, :] = peak
    stats[1:2, :] = jnp.sum(jnp.exp(value - peak), axis=0, keepdims=True)
    stats[2:3, :] = jnp.sum(jnp.where(rows == labels[...], value, 0.0), axis=0, keepdims=True)


def grad_kernel(pos, own_far, other_far, logits, labels, loss_weight, stats,
                grad, a0, a1, a2, a3, b0, b1, b2, b3,
                grad_t, part_own, part_other, own, other, sems):
    copies = fetch(own_far, other_far, own, other, sems)
    value = logits[...]
    rows = lax.broadcasted_iota(jnp.int32, value.shape, 0) + pos[3]
    target = jnp.where(rows == labels[...], 1.0, 0.0)
    result = loss_weight[...] * (jnp.exp(value - stats[0:1, :]) / stats[1:2, :] - target)
    grad[...] = result.astype(BF)
    grad_t[...] = result.T.astype(BF)
    width = own.shape[1] // 2
    for j in range(4):
        if j % 2 == 0:
            copies[j // 2].wait()
        weight, part = (own, part_own) if j < 2 else (other, part_other)
        span = slice((j % 2) * width, (j % 2 + 1) * width)
        piece = jnp.dot(grad_t[...], weight[:, span], preferred_element_type=F32)
        part[span, :] = piece.T.astype(BF)

    def take(piece, index, half, rows):
        piece[index] = half[rows, :]

    firsts, seconds = (a0, a1, a2, a3), (b0, b1, b2, b3)
    each_piece(pos, a0.shape[2], firsts, seconds, part_own, part_other, take)


def per_device(hidden, head_weight, labels, loss_weight):
    rows, half = head_weight.shape
    tokens, cols = hidden.shape
    side = 2 * cols
    swap = [(0, 1), (1, 0)]
    weight_other = lax.ppermute(head_weight, "dp", swap)
    pos = jnp.stack(
        [lax.axis_index("dp"), lax.axis_index("x"), lax.axis_index("y"),
         lax.axis_index(SECTIONS) * rows]
    ).astype(jnp.int32)
    labels = labels[None, :]
    loss_weight = loss_weight[None, :]
    params = pltpu.CompilerParams(vmem_limit_bytes=50 * 1024 * 1024)
    weights = [pltpu.VMEM((rows, half), BF)] * 2 + [pltpu.SemaphoreType.DMA((2,))]

    line = share(hidden.T, ("zh", "t")).reshape(2, 2, side, tokens)
    first = jnp.stack(spread(line[:, 0], "x"))
    second = jnp.stack(spread(line[:, 1], "y"))
    first, second, weight_other = lax.optimization_barrier((first, second, weight_other))
    first = spread(first, "y")
    second = spread(second, "x")
    logits, stats, feats_own, feats_other = pl.pallas_call(
        logits_kernel,
        in_specs=[SMEM] + [HBM] * 2 + [VMEM] * 9,
        out_specs=[VMEM] * 4,
        out_shape=[
            jax.ShapeDtypeStruct((rows, tokens), F32),
            jax.ShapeDtypeStruct((3, tokens), F32),
            jax.ShapeDtypeStruct((half, tokens), BF),
            jax.ShapeDtypeStruct((half, tokens), BF),
        ],
        scratch_shapes=weights,
        compiler_params=params,
        name="logits",
    )(pos, head_weight, weight_other, labels, *first, *second)

    stats = combine(share(stats, ("x", "y", "t")))
    stats, feats_other = lax.optimization_barrier((stats, feats_other))
    feats_peer = lax.ppermute(feats_other, "dp", swap)
    stats = combine(jnp.stack([stats, lax.ppermute(stats, "zh", swap)]))
    token_loss = stats[0] + jnp.log(stats[1]) - stats[2]

    outs = pl.pallas_call(
        grad_kernel,
        in_specs=[SMEM] + [HBM] * 2 + [VMEM] * 4,
        out_specs=[VMEM] * 9,
        out_shape=[jax.ShapeDtypeStruct((rows, tokens), BF)]
        + [jax.ShapeDtypeStruct(first[0].shape, BF)] * 8,
        scratch_shapes=[
            pltpu.VMEM((tokens, rows), BF),
            pltpu.VMEM((half, tokens), BF),
            pltpu.VMEM((half, tokens), BF),
        ] + weights,
        compiler_params=params,
        name="grads",
    )(pos, head_weight, weight_other, logits, labels, loss_weight, stats)
    grad = outs[0]

    first = collect(outs[1:5], "y").astype(BF)
    second = collect(outs[5:9], "x").astype(BF)
    first, second, grad = lax.optimization_barrier((first, second, grad))
    grad_peer = lax.ppermute(grad, "dp", swap)
    dot = lambda a, b: lax.dot_general(
        a, b, (((1,), (1,)), ((), ())), preferred_element_type=F32
    )
    head_grad = (dot(grad, feats_own) + dot(grad_peer, feats_peer)).astype(BF)
    first = collect([first[k] for k in range(4)], "x")
    second = collect([second[k] for k in range(4)], "y")
    line = jnp.concatenate([first, second], axis=1).reshape(8, cols, tokens)
    line = lax.all_to_all(line, ("zh", "t"), 0, 0)
    line, head_grad = lax.optimization_barrier((line, head_grad))
    line = jnp.sum(line, axis=0)
    return (line.astype(BF).T, head_grad, token_loss)


def solution(mesh):
    fine = Mesh(mesh.devices.reshape(4, 2, 4, 4, 2), ("x", "zh", "y", "t", "dp"))
    return jax.shard_map(
        per_device,
        mesh=fine,
        in_specs=(P("dp", SECTIONS), P(SECTIONS, "dp"), P("dp"), P("dp")),
        out_specs=(P("dp", SECTIONS), P(SECTIONS, "dp"), P("dp")),
        check_vma=False,
    )
```

```python
import jax
import jax.numpy as jnp
from jax import lax
from jax.experimental import pallas as pl
from jax.experimental.pallas import tpu as pltpu
from jax.sharding import Mesh, PartitionSpec as P

BF = jnp.bfloat16
F32 = jnp.float32
HBM = pl.BlockSpec(memory_space=pltpu.HBM)
VMEM = pl.BlockSpec(memory_space=pltpu.VMEM)
SMEM = pl.BlockSpec(memory_space=pltpu.SMEM)
SECTIONS = ("x", "zh", "y", "t")


def paired(n, k):
    return [(i, i ^ k) for i in range(n)]


def spread(block, axis):
    got = {k: lax.ppermute(block, axis, paired(4, k)) for k in (2, 1, 3)}
    got[0] = block
    return [got[k] for k in range(4)]


def collect(blocks, axis):
    got = [lax.ppermute(blocks[k], axis, paired(4, k)) for k in (2, 1, 3)]
    total = blocks[0].astype(F32)
    for piece in got:
        total = total + piece.astype(F32)
    return total


def share(block, axes):
    n = lax.axis_size(axes)
    return lax.all_to_all(jnp.broadcast_to(block[None], (n,) + block.shape), axes, 0, 0)


def combine(every):
    peak = jnp.max(every[:, 0], axis=0)
    total = jnp.sum(every[:, 1] * jnp.exp(every[:, 0] - peak[None]), axis=0)
    return jnp.stack([peak, total, jnp.sum(every[:, 2], axis=0)])


def each_piece(pos, side, firsts, seconds, own, other, act):
    core, x, y = pos[0], pos[1], pos[2]
    for kx in range(4):
        place = x ^ kx ^ (2 * core)

        def visit(half):
            for zh in range(2):
                for ky in range(4):
                    block = ((place % 2) * 2 + zh) * 4 + (y ^ ky)
                    row = pl.multiple_of(block * 2 * side, 16)
                    act(firsts[ky], (kx, zh), half, pl.ds(row, side))
                    row = pl.multiple_of(block * 2 * side + side, 16)
                    act(seconds[kx], (ky, zh), half, pl.ds(row, side))

        pl.when(place < 2)(lambda: visit(own))
        pl.when(place >= 2)(lambda: visit(other))


def fetch(own_far, other_far, own, other, sems):
    width = own.shape[1] // 2
    copies = []
    for j in range(4):
        far, near = (own_far, own) if j < 2 else (other_far, other)
        span = pl.ds((j % 2) * width, width)
        copies.append(pltpu.make_async_copy(far.at[:, span], near.at[:, span], sems.at[j]))
        copies[-1].start()
    return copies


def logits_kernel(pos, own_far, other_far, labels, a0, a1, a2, a3, b0, b1, b2, b3,
                  logits, stats, feats_own, feats_other, own, other, sems):
    copies = fetch(own_far, other_far, own, other, sems)

    def place(piece, index, half, rows):
        half[rows, :] = piece[index]

    firsts, seconds = (a0, a1, a2, a3), (b0, b1, b2, b3)
    each_piece(pos, a0.shape[2], firsts, seconds, feats_own, feats_other, place)
    copies[0].wait()
    copies[1].wait()
    logits[...] = jnp.dot(own[...], feats_own[...], preferred_element_type=F32)
    width = own.shape[1] // 2
    for j in range(2):
        copies[2 + j].wait()
        span = slice(j * width, (j + 1) * width)
        logits[...] += jnp.dot(other[:, span], feats_other[span], preferred_element_type=F32)
    value = logits[...]
    rows = lax.broadcasted_iota(jnp.int32, value.shape, 0) + pos[3]
    peak = jnp.max(value, axis=0, keepdims=True)
    stats[0:1, :] = peak
    stats[1:2, :] = jnp.sum(jnp.exp(value - peak), axis=0, keepdims=True)
    stats[2:3, :] = jnp.sum(jnp.where(rows == labels[...], value, 0.0), axis=0, keepdims=True)


def grad_kernel(pos, own_far, other_far, logits, labels, loss_weight, stats,
                grad, a0, a1, a2, a3, b0, b1, b2, b3,
                grad_t, part_own, part_other, own, other, sems):
    copies = fetch(own_far, other_far, own, other, sems)
    value = logits[...]
    rows = lax.broadcasted_iota(jnp.int32, value.shape, 0) + pos[3]
    target = jnp.where(rows == labels[...], 1.0, 0.0)
    result = loss_weight[...] * (jnp.exp(value - stats[0:1, :]) / stats[1:2, :] - target)
    grad[...] = result.astype(BF)
    grad_t[...] = result.T.astype(BF)
    width = own.shape[1] // 2
    for j in range(4):
        copies[j].wait()
        weight, part = (own, part_own) if j < 2 else (other, part_other)
        span = slice((j % 2) * width, (j % 2 + 1) * width)
        piece = jnp.dot(grad_t[...], weight[:, span], preferred_element_type=F32)
        part[span, :] = piece.T.astype(BF)

    def take(piece, index, half, rows):
        piece[index] = half[rows, :]

    firsts, seconds = (a0, a1, a2, a3), (b0, b1, b2, b3)
    each_piece(pos, a0.shape[2], firsts, seconds, part_own, part_other, take)


def per_device(hidden, head_weight, labels, loss_weight):
    rows, half = head_weight.shape
    tokens, cols = hidden.shape
    side = 2 * cols
    swap = [(0, 1), (1, 0)]
    weight_other = lax.ppermute(head_weight, "dp", swap)
    pos = jnp.stack(
        [lax.axis_index("dp"), lax.axis_index("x"), lax.axis_index("y"),
         lax.axis_index(SECTIONS) * rows]
    ).astype(jnp.int32)
    labels = labels[None, :]
    loss_weight = loss_weight[None, :]
    params = pltpu.CompilerParams(vmem_limit_bytes=42 * 1024 * 1024)
    weights = [pltpu.VMEM((rows, half), BF)] * 2 + [pltpu.SemaphoreType.DMA((4,))]

    line = share(hidden.T, ("zh", "t")).reshape(2, 2, side, tokens)
    first = jnp.stack(spread(line[:, 0], "x"))
    second = jnp.stack(spread(line[:, 1], "y"))
    first, second, weight_other = lax.optimization_barrier((first, second, weight_other))
    first = spread(first, "y")
    second = spread(second, "x")
    logits, stats, feats_own, feats_other = pl.pallas_call(
        logits_kernel,
        in_specs=[SMEM] + [HBM] * 2 + [VMEM] * 9,
        out_specs=[VMEM] * 4,
        out_shape=[
            jax.ShapeDtypeStruct((rows, tokens), F32),
            jax.ShapeDtypeStruct((3, tokens), F32),
            jax.ShapeDtypeStruct((half, tokens), BF),
            jax.ShapeDtypeStruct((half, tokens), BF),
        ],
        scratch_shapes=weights,
        compiler_params=pltpu.CompilerParams(vmem_limit_bytes=50 * 1024 * 1024),
        name="logits",
    )(pos, head_weight, weight_other, labels, *first, *second)

    stats = combine(share(stats, ("x", "y", "t")))
    stats, feats_other = lax.optimization_barrier((stats, feats_other))
    feats_peer = lax.ppermute(feats_other, "dp", swap)
    stats = combine(jnp.stack([stats, lax.ppermute(stats, "zh", swap)]))
    token_loss = stats[0] + jnp.log(stats[1]) - stats[2]

    outs = pl.pallas_call(
        grad_kernel,
        in_specs=[SMEM] + [HBM] * 2 + [VMEM] * 4,
        out_specs=[VMEM] * 9,
        out_shape=[jax.ShapeDtypeStruct((rows, tokens), BF)]
        + [jax.ShapeDtypeStruct(first[0].shape, BF)] * 8,
        scratch_shapes=[
            pltpu.VMEM((tokens, rows), BF),
            pltpu.VMEM((half, tokens), BF),
            pltpu.VMEM((half, tokens), BF),
        ] + weights,
        compiler_params=params,
        name="grads",
    )(pos, head_weight, weight_other, logits, labels, loss_weight, stats)
    grad = outs[0]

    first = collect(outs[1:5], "y").astype(BF)
    second = collect(outs[5:9], "x").astype(BF)
    first, second, grad = lax.optimization_barrier((first, second, grad))
    grad_peer = lax.ppermute(grad, "dp", swap)
    dot = lambda a, b: lax.dot_general(
        a, b, (((1,), (1,)), ((), ())), preferred_element_type=F32
    )
    head_grad = (dot(grad, feats_own) + dot(grad_peer, feats_peer)).astype(BF)
    first = collect([first[k] for k in range(4)], "x")
    second = collect([second[k] for k in range(4)], "y")
    line = jnp.concatenate([first, second], axis=1).reshape(8, cols, tokens)
    line = lax.all_to_all(line, ("zh", "t"), 0, 0)
    line, head_grad = lax.optimization_barrier((line, head_grad))
    line = jnp.sum(line, axis=0)
    return (line.astype(BF).T, head_grad, token_loss)


def solution(mesh):
    fine = Mesh(mesh.devices.reshape(4, 2, 4, 4, 2), ("x", "zh", "y", "t", "dp"))
    return jax.shard_map(
        per_device,
        mesh=fine,
        in_specs=(P("dp", SECTIONS), P(SECTIONS, "dp"), P("dp"), P("dp")),
        out_specs=(P("dp", SECTIONS), P(SECTIONS, "dp"), P("dp")),
        check_vma=False,
    )
```

```python
import jax
import jax.numpy as jnp
from jax import lax
from jax.experimental import pallas as pl
from jax.experimental.pallas import tpu as pltpu
from jax.sharding import Mesh, PartitionSpec as P

BF = jnp.bfloat16
F32 = jnp.float32
HBM = pl.BlockSpec(memory_space=pltpu.HBM)
VMEM = pl.BlockSpec(memory_space=pltpu.VMEM)
SMEM = pl.BlockSpec(memory_space=pltpu.SMEM)
SECTIONS = ("x", "zh", "y", "t")


def paired(n, k):
    return [(i, i ^ k) for i in range(n)]


def spread(block, axis):
    got = {k: lax.ppermute(block, axis, paired(4, k)) for k in (2, 1, 3)}
    got[0] = block
    return [got[k] for k in range(4)]


def collect(blocks, axis):
    got = [lax.ppermute(blocks[k], axis, paired(4, k)) for k in (2, 1, 3)]
    total = blocks[0].astype(F32)
    for piece in got:
        total = total + piece.astype(F32)
    return total


def share(block, axes):
    n = lax.axis_size(axes)
    return lax.all_to_all(jnp.broadcast_to(block[None], (n,) + block.shape), axes, 0, 0)


def combine(every):
    peak = jnp.max(every[:, 0], axis=0)
    total = jnp.sum(every[:, 1] * jnp.exp(every[:, 0] - peak[None]), axis=0)
    return jnp.stack([peak, total, jnp.sum(every[:, 2], axis=0)])


def each_piece(pos, side, firsts, seconds, own, other, act):
    core, x, y = pos[0], pos[1], pos[2]
    for kx in range(4):
        place = x ^ kx ^ (2 * core)

        def visit(half):
            for zh in range(2):
                for ky in range(4):
                    block = ((place % 2) * 2 + zh) * 4 + (y ^ ky)
                    row = pl.multiple_of(block * 2 * side, 16)
                    act(firsts[ky], (kx, zh), half, pl.ds(row, side))
                    row = pl.multiple_of(block * 2 * side + side, 16)
                    act(seconds[kx], (ky, zh), half, pl.ds(row, side))

        if own is not None:
            pl.when(place < 2)(lambda: visit(own))
        if other is not None:
            pl.when(place >= 2)(lambda: visit(other))


def fetch(own_far, other_far, own, other, sems):
    width = own.shape[1] // 2
    copies = []
    for j in range(4):
        far, near = (own_far, own) if j < 2 else (other_far, other)
        span = pl.ds((j % 2) * width, width)
        copies.append(pltpu.make_async_copy(far.at[:, span], near.at[:, span], sems.at[j]))
        copies[-1].start()
    return copies


def logits_kernel(pos, own_far, other_far, labels, a0, a1, a2, a3, b0, b1, b2, b3,
                  logits, stats, own_out, other_out, own, other, sems,
                  feats_own, feats_other, out_sems):
    copies = fetch(own_far, other_far, own, other, sems)

    def place(piece, index, half, rows):
        half[rows, :] = piece[index]

    firsts, seconds = (a0, a1, a2, a3), (b0, b1, b2, b3)
    each_piece(pos, a0.shape[2], firsts, seconds, feats_own, feats_other, place)
    leaving = [
        pltpu.make_async_copy(feats_own, own_out, out_sems.at[0]),
        pltpu.make_async_copy(feats_other, other_out, out_sems.at[1]),
    ]
    for copy in leaving:
        copy.start()
    copies[0].wait()
    copies[1].wait()
    logits[...] = jnp.dot(own[...], feats_own[...], preferred_element_type=F32)
    width = own.shape[1] // 2
    for j in range(2):
        copies[2 + j].wait()
        span = slice(j * width, (j + 1) * width)
        logits[...] += jnp.dot(other[:, span], feats_other[span], preferred_element_type=F32)
    value = logits[...]
    rows = lax.broadcasted_iota(jnp.int32, value.shape, 0) + pos[3]
    peak = jnp.max(value, axis=0, keepdims=True)
    stats[0:1, :] = peak
    stats[1:2, :] = jnp.sum(jnp.exp(value - peak), axis=0, keepdims=True)
    stats[2:3, :] = jnp.sum(jnp.where(rows == labels[...], value, 0.0), axis=0, keepdims=True)
    for copy in leaving:
        copy.wait()


def grad_kernel(pos, own_far, other_far, logits, labels, loss_weight, stats,
                grad, a0, a1, a2, a3, b0, b1, b2, b3,
                grad_t, part_own, part_other, own, other, sems):
    copies = fetch(own_far, other_far, own, other, sems)
    value = logits[...]
    rows = lax.broadcasted_iota(jnp.int32, value.shape, 0) + pos[3]
    target = jnp.where(rows == labels[...], 1.0, 0.0)
    result = loss_weight[...] * (jnp.exp(value - stats[0:1, :]) / stats[1:2, :] - target)
    grad[...] = result.astype(BF)
    grad_t[...] = result.T.astype(BF)
    width = own.shape[1] // 2
    firsts, seconds = (a0, a1, a2, a3), (b0, b1, b2, b3)

    def take(piece, index, half, rows):
        piece[index] = half[rows, :]

    for j in range(4):
        copies[j].wait()
        weight, part = (own, part_own) if j < 2 else (other, part_other)
        span = slice((j % 2) * width, (j % 2 + 1) * width)
        piece = jnp.dot(grad_t[...], weight[:, span], preferred_element_type=F32)
        part[span, :] = piece.T.astype(BF)
        if j == 1:
            each_piece(pos, a0.shape[2], firsts, seconds, part_own, None, take)
    each_piece(pos, a0.shape[2], firsts, seconds, None, part_other, take)


def per_device(hidden, head_weight, labels, loss_weight):
    rows, half = head_weight.shape
    tokens, cols = hidden.shape
    side = 2 * cols
    swap = [(0, 1), (1, 0)]
    weight_other = lax.ppermute(head_weight, "dp", swap)
    pos = jnp.stack(
        [lax.axis_index("dp"), lax.axis_index("x"), lax.axis_index("y"),
         lax.axis_index(SECTIONS) * rows]
    ).astype(jnp.int32)
    labels = labels[None, :]
    loss_weight = loss_weight[None, :]
    params = pltpu.CompilerParams(vmem_limit_bytes=42 * 1024 * 1024)
    weights = [pltpu.VMEM((rows, half), BF)] * 2 + [pltpu.SemaphoreType.DMA((4,))]

    line = share(hidden.T, ("zh", "t")).reshape(2, 2, side, tokens)
    first = jnp.stack(spread(line[:, 0], "x"))
    second = jnp.stack(spread(line[:, 1], "y"))
    first, second, weight_other = lax.optimization_barrier((first, second, weight_other))
    first = spread(first, "y")
    second = spread(second, "x")
    logits, stats, feats_own, feats_other = pl.pallas_call(
        logits_kernel,
        in_specs=[SMEM] + [HBM] * 2 + [VMEM] * 9,
        out_specs=[VMEM] * 2 + [HBM] * 2,
        out_shape=[
            jax.ShapeDtypeStruct((rows, tokens), F32),
            jax.ShapeDtypeStruct((3, tokens), F32),
            jax.ShapeDtypeStruct((half, tokens), BF),
            jax.ShapeDtypeStruct((half, tokens), BF),
        ],
        scratch_shapes=weights
        + [pltpu.VMEM((half, tokens), BF)] * 2
        + [pltpu.SemaphoreType.DMA((2,))],
        compiler_params=pltpu.CompilerParams(vmem_limit_bytes=50 * 1024 * 1024),
        name="logits",
    )(pos, head_weight, weight_other, labels, *first, *second)

    stats = combine(share(stats, ("x", "y", "t")))
    stats, feats_other = lax.optimization_barrier((stats, feats_other))
    feats_peer = lax.ppermute(feats_other, "dp", swap)
    stats = combine(jnp.stack([stats, lax.ppermute(stats, "zh", swap)]))
    token_loss = stats[0] + jnp.log(stats[1]) - stats[2]

    outs = pl.pallas_call(
        grad_kernel,
        in_specs=[SMEM] + [HBM] * 2 + [VMEM] * 4,
        out_specs=[VMEM] * 9,
        out_shape=[jax.ShapeDtypeStruct((rows, tokens), BF)]
        + [jax.ShapeDtypeStruct(first[0].shape, BF)] * 8,
        scratch_shapes=[
            pltpu.VMEM((tokens, rows), BF),
            pltpu.VMEM((half, tokens), BF),
            pltpu.VMEM((half, tokens), BF),
        ] + weights,
        compiler_params=params,
        name="grads",
    )(pos, head_weight, weight_other, logits, labels, loss_weight, stats)
    grad = outs[0]

    first = collect(outs[1:5], "y").astype(BF)
    second = collect(outs[5:9], "x").astype(BF)
    first, second, grad = lax.optimization_barrier((first, second, grad))
    grad_peer = lax.ppermute(grad, "dp", swap)
    dot = lambda a, b: lax.dot_general(
        a, b, (((1,), (1,)), ((), ())), preferred_element_type=F32
    )
    head_grad = (dot(grad, feats_own) + dot(grad_peer, feats_peer)).astype(BF)
    first = collect([first[k] for k in range(4)], "x")
    second = collect([second[k] for k in range(4)], "y")
    line = jnp.concatenate([first, second], axis=1).reshape(8, cols, tokens)
    line = lax.all_to_all(line, ("zh", "t"), 0, 0)
    line, head_grad = lax.optimization_barrier((line, head_grad))
    line = jnp.sum(line, axis=0)
    return (line.astype(BF).T, head_grad, token_loss)


def solution(mesh):
    fine = Mesh(mesh.devices.reshape(4, 2, 4, 4, 2), ("x", "zh", "y", "t", "dp"))
    return jax.shard_map(
        per_device,
        mesh=fine,
        in_specs=(P("dp", SECTIONS), P(SECTIONS, "dp"), P("dp"), P("dp")),
        out_specs=(P("dp", SECTIONS), P(SECTIONS, "dp"), P("dp")),
        check_vma=False,
    )
```
